32 devices in a mesh: seq: 8 (over y, x, core), chan: 4 (over z).
Axes of the slice: x: 2, y: 2, z: 4, core: 2. Of those that a mesh axis runs over, the one named last changes fastest.
Arguments:
- residual: bfloat16 [1024, 8192], P('seq', 'chan'), may hold values from -64 to 64
- query_in: bfloat16 [1024, 8192], P('seq', 'chan'), may hold values from -6 to 6
- key_in: bfloat16 [1024, 8192], P('seq', 'chan'), may hold values from -6 to 6
- value_in: bfloat16 [1024, 8192], P('seq', 'chan'), may hold values from -6 to 6
- short_filter: float32 [3, 3, 8192], P(None, None, 'chan'), may hold values from -3.5 to 3.5
- decay_rate: float32 [16, 8192], P(None, 'chan'), may hold values from 0 to 1
- residue: float32 [16, 8192], P(None, 'chan'), may hold values from -1.5 to 1.5
- skip_gain: float32 [8192], P('chan'), may hold values from -3 to 3
- norm_gain: float32 [8192], P('chan'), may hold values from 0.1 to 1.9
Outputs:
- residual_out: bfloat16 [1024, 8192], P('seq', 'chan')
- normed: bfloat16 [1024, 8192], P('seq', 'chan')
The draws below stay inside these ranges and needn't reach their ends.
All inputs are finite; a program needn't handle non-finite values.
Results may differ from the reference program's by a relative error of at most 0.0055.
Values may be sent and summed in bfloat16 or wider, within the bound.
A program may use at most 128 MiB of HBM per device.

```python
import math
import jax
import jax.numpy as jnp
from jax import lax

D = 8192
POLES = 16
SHORT = 3
SEQ_LEN = 1024


def draw_decay_rate(key, part):
    first = jax.random.fold_in(key, 0)
    lowest = math.log(0.3 / SEQ_LEN)
    highest = math.log(1.0 / 16.0)
    spread = jax.random.uniform(first, (POLES, D), jnp.float32, lowest, highest)
    return jnp.exp(spread).astype(jnp.float32)


def draw_residual(key, part):
    first, second, third = jax.random.split(key, 3)
    row_scale = jnp.exp(jax.random.uniform(first, (SEQ_LEN, 1), jnp.float32, math.log(0.3), math.log(3.0)))
    column_scale = jnp.exp(jax.random.uniform(second, (1, D), jnp.float32, math.log(0.3), math.log(3.0)))
    along = jnp.arange(D, dtype=jnp.float32)[None, :] / max(D - 1, 1)
    base = jnp.clip(jax.random.normal(third, (SEQ_LEN, D), jnp.float32), -4.0, 4.0)
    ramp = jnp.exp(0.5 * math.log(3.0) * along)
    return (base * row_scale * column_scale * ramp).astype(jnp.bfloat16)


def levels(key, dims, cuts, low, largest):
    def one(position, parts):
        draws = jax.random.uniform(jax.random.fold_in(jax.random.fold_in(key, 6), position), (parts,), jnp.float32, low / len(cuts), largest / len(cuts))
        return jnp.repeat(jnp.exp(draws), dims[position] // parts).reshape((-1,) + (1,) * (len(dims) - position - 1))

    gain = one(*cuts[0])
    for cut in cuts[1:]:
        gain = gain * one(*cut)
    return gain


def gaussian(own_key, dims, scale, bound, shards=(), kind=jnp.bfloat16):
    array = scale * jax.random.normal(own_key, dims, jnp.float32)
    if shards:
        array = array * levels(own_key, dims, shards, -0.22, 0.18)
    return jnp.clip(array, -bound, bound).astype(kind)


def setup_inputs(seed: int = 0) -> dict:
    key_of = jax.random.split(jax.random.key(seed), 10)
    return {
        "residual": draw_residual(jax.random.fold_in(key_of[9], 71), 0),
        "query_in": gaussian(key_of[1], (SEQ_LEN, D), 1.0, 6.0, ((0, 8), (1, 4))),
        "key_in": gaussian(key_of[2], (SEQ_LEN, D), 1.0, 6.0, ((0, 8), (1, 4))),
        "value_in": gaussian(key_of[3], (SEQ_LEN, D), 1.0, 6.0, ((0, 8), (1, 4))),
        "short_filter": gaussian(key_of[4], (3, SHORT, D), SHORT ** -0.5, 3.5, ((2, 4),), jnp.float32),
        "decay_rate": draw_decay_rate(jax.random.fold_in(key_of[9], 71), 0),
        "residue": gaussian(key_of[6], (POLES, D), 0.25, 1.5, ((1, 4),), jnp.float32),
        "skip_gain": gaussian(key_of[7], (D,), 0.5, 3.0, ((0, 4),), jnp.float32),
        "norm_gain": jnp.clip(1.0 + 0.18 * jax.random.normal(key_of[8], (D,), jnp.float32), 0.1, 1.9),
    }


def reference(residual, query_in, key_in, value_in, short_filter, decay_rate, residue, skip_gain, norm_gain):
    lag_rows = SHORT - 1
    filters = short_filter.astype(jnp.float32)
    decays = decay_rate.astype(jnp.float32)
    factor = jnp.exp(-decays)
    weights = residue.astype(jnp.float32) * jnp.sqrt(2.0 * decays)
    direct = skip_gain.astype(jnp.float32)
    gains = norm_gain.astype(jnp.float32)

    def advance(carried, inputs):
        previous, state = carried
        stream_row, query_row, key_row, value_row = inputs
        current = jnp.stack([query_row, key_row, value_row]).astype(jnp.float32)
        window = jnp.concatenate([current[:, None, :], previous], axis=1)
        features = lax.optimization_barrier(jnp.sum(filters * window, axis=1))
        mixed = features[1] * features[2]
        state = factor * state + mixed[None, :]
        convolved = lax.optimization_barrier(jnp.sum(weights * state, axis=0))
        gated = features[0] * (convolved + direct * mixed)
        summed = (stream_row.astype(jnp.float32) + gated).astype(jnp.bfloat16)
        widened = lax.optimization_barrier(summed).astype(jnp.float32)
        inverse_rms = lax.rsqrt(jnp.mean(widened * widened) + 1e-06)
        normed = (widened * inverse_rms * gains).astype(jnp.bfloat16)
        return ((window[:, :lag_rows, :], state), (summed, normed))
    initial = (jnp.zeros((3, lag_rows, D), jnp.float32), jnp.zeros((POLES, D), jnp.float32))
    _, outputs = lax.scan(advance, initial, (residual, query_in, key_in, value_in))
    return (outputs[0], outputs[1])
```

```python
import functools

import jax
import jax.numpy as jnp
from jax import lax
from jax.experimental import pallas as pl
from jax.experimental.pallas import tpu as pltpu
from jax.sharding import PartitionSpec as P

D = 8192
LANES = 128
epsilon = 1e-06
MESH = pl.DeviceIdType.MESH


def tree_sum(terms):
    while len(terms) > 1:
        paired = [terms[i] + terms[i + 1] for i in range(0, len(terms) - 1, 2)]
        if len(terms) % 2:
            paired.append(terms[-1])
        terms = paired
    return terms[0]


def kernel(
    seq_size,
    chan_size,
    residual_ref,
    query_ref,
    key_ref,
    value_ref,
    filter_ref,
    decay_ref,
    residue_ref,
    skip_ref,
    gain_ref,
    summed_ref,
    normed_ref,
    mix_ref,
    conv_ref,
    query_side_ref,
    stage_ref,
    rate_ref,
    factor_ref,
    weight_ref,
    total_ref,
    carried_ref,
    tail_out,
    tail_in,
    state_out,
    state_in,
    squares_ref,
    squares_out,
    squares_in,
    tail_sem,
    state_send,
    state_recv,
    chan_send,
    chan_recv,
):
    rows, width = residual_ref.shape
    poles = decay_ref.shape[0]
    groups = width // LANES
    halves = groups // 8
    pitch = rows + 8
    levels = seq_size.bit_length() - 1
    me = lax.axis_index("seq")
    my_chan = lax.axis_index("chan")
    after = lax.rem(me + 1, seq_size)
    previous = lax.rem(me + seq_size - 1, seq_size)
    partners = [
        me + (1 - 2 * lax.rem(lax.div(me, 1 << k), 2)) * (1 << k) for k in range(levels)
    ]
    chan_peers = [lax.rem(my_chan + j, chan_size) for j in range(1, chan_size)]

    barrier = pltpu.get_barrier_semaphore()
    for other in [after, previous] + partners:
        pl.semaphore_signal(barrier, inc=1, device_id={"seq": other}, device_id_type=MESH)
    for other in chan_peers:
        pl.semaphore_signal(barrier, inc=1, device_id={"chan": other}, device_id_type=MESH)

    inputs = (query_ref, key_ref, value_ref)
    for i in range(3):
        last = inputs[i][rows - 16 : rows, :].astype(jnp.float32)
        tail_out[2 * i : 2 * i + 2, :] = last[14:16, :]
    tail_out[6:8, :] = jnp.zeros((2, width), jnp.float32)
    pl.semaphore_wait(barrier, 2 + levels + chan_size - 1)
    tail_copy = pltpu.make_async_remote_copy(
        src_ref=tail_out,
        dst_ref=tail_in,
        send_sem=tail_sem.at[0],
        recv_sem=tail_sem.at[1],
        device_id={"seq": after},
        device_id_type=MESH,
    )
    tail_copy.start()

    def to_channels(source, target):
        for g in range(groups):
            stage_ref[g * poles : (g + 1) * poles, :] = source[:, g * LANES : (g + 1) * LANES]
        for p in range(poles):
            for h in range(halves):
                target[p, h * 8 : h * 8 + 8, :] = stage_ref[
                    pl.ds(h * 8 * poles + p, 8, stride=poles), :
                ]

    to_channels(decay_ref, rate_ref)
    to_channels(residue_ref, weight_ref)
    rate = rate_ref[...]
    factor_ref[...] = jnp.exp(-rate)
    weight_ref[...] = weight_ref[...] * jnp.sqrt(2.0 * rate)

    def feature(i, count, lanes, tail):
        block = inputs[i][0:count, lanes].astype(jnp.float32)
        once = pltpu.roll(block, 1, 0)
        twice = pltpu.roll(block, 2, 0)
        if tail is not None:
            row = lax.broadcasted_iota(jnp.int32, (count, LANES), 0)
            older = tail[2 * i : 2 * i + 1, :]
            newer = tail[2 * i + 1 : 2 * i + 2, :]
            once = jnp.where(row == 0, newer, once)
            twice = jnp.where(row == 0, older, jnp.where(row == 1, newer, twice))
        taps = filter_ref[i, :, lanes]
        return taps[0:1, :] * block + taps[1:2, :] * once + taps[2:3, :] * twice

    def lanes_of(g):
        return pl.ds(pl.multiple_of(g * LANES, LANES), LANES)

    def place_of(g, count):
        return pl.ds(pl.multiple_of(g * pitch, 8), count)

    def mix_all(g, _):
        lanes = lanes_of(g)
        mix_ref[place_of(g, rows), :] = feature(1, rows, lanes, None) * feature(
            2, rows, lanes, None
        )
        return 0

    lax.fori_loop(0, groups, mix_all, 0)
    tail_copy.wait()
    is_first = me == 0

    def mix_first(g, _):
        lanes = lanes_of(g)
        tail = jnp.where(is_first, 0.0, tail_in[:, lanes])
        product = feature(1, 16, lanes, tail) * feature(2, 16, lanes, tail)
        mix_ref[place_of(g, 8), :] = product[0:8, :]
        return 0

    lax.fori_loop(0, groups, mix_first, 0)

    def half_of(ref, h):
        return tuple(ref[p, h * 8 : h * 8 + 8, :] for p in range(poles))

    def token(h, t):
        return pl.ds(h * 8 * pitch + t, 8, stride=pitch)

    zeros = (jnp.zeros((8, LANES), jnp.float32),) * poles
    for h in range(halves):
        factor = half_of(factor_ref, h)

        def advance(t, state, h=h, factor=factor):
            current = mix_ref[token(h, t), :]
            return tuple(a * s + current for a, s in zip(factor, state))

        state = lax.fori_loop(0, rows, advance, zeros, unroll=8)
        for p in range(poles):
            total_ref[p, h * 8 : h * 8 + 8, :] = state[p]

    def state_copy(k):
        return pltpu.make_async_remote_copy(
            src_ref=state_out.at[k],
            dst_ref=state_in.at[k],
            send_sem=state_send.at[k],
            recv_sem=state_recv.at[k],
            device_id={"seq": partners[k]},
            device_id_type=MESH,
        )

    def query_all(g, _):
        lanes = lanes_of(g)
        tail = jnp.where(is_first, 0.0, tail_in[:, lanes])
        query_side_ref[:, lanes] = feature(0, rows, lanes, tail)
        return 0

    def local_half(h):
        factor = half_of(factor_ref, h)

        def advance(t, state):
            current = mix_ref[token(h, t), :]
            state = tuple(a * s + current for a, s in zip(factor, state))
            conv_ref[token(h, t), :] = tree_sum(
                [weight_ref[p, h * 8 : h * 8 + 8, :] * state[p] for p in range(poles)]
            )
            return state

        lax.fori_loop(0, rows, advance, zeros, unroll=8)

    beside = {0: [lambda: lax.fori_loop(0, groups, query_all, 0)]}
    for h in range(halves):
        beside.setdefault(min(1 + h, levels - 1), []).append(functools.partial(local_half, h))
    carried_ref[...] = jnp.zeros_like(carried_ref)
    for k in range(levels):
        state_out[k] = total_ref[...].astype(jnp.bfloat16)
        copy = state_copy(k)
        copy.start()
        for work in beside.get(k, []):
            work()
        copy.wait()
        size = 1 << k
        inside = lax.rem(me, size)
        upper = lax.rem(lax.div(me, size), 2) == 1
        span = (rows * inside).astype(jnp.float32)
        rate = rate_ref[...]
        arrived = state_in[k].astype(jnp.float32)
        carried_ref[...] += jnp.where(upper, jnp.exp(-rate * span) * arrived, 0.0)
        if k < levels - 1:
            own = total_ref[...]
            early = jnp.where(upper, arrived, own)
            late = jnp.where(upper, own, arrived)
            total_ref[...] = late + jnp.exp(-rate * (rows * size)) * early

    for h in range(halves):
        factor = half_of(factor_ref, h)
        start = tuple(
            weight_ref[p, h * 8 : h * 8 + 8, :] * carried_ref[p, h * 8 : h * 8 + 8, :]
            for p in range(poles)
        )

        def across(t, state, h=h, factor=factor):
            state = tuple(a * s for a, s in zip(factor, state))
            conv_ref[token(h, t), :] = conv_ref[token(h, t), :] + tree_sum(list(state))
            return state

        lax.fori_loop(0, rows, across, start, unroll=8)

    padded = squares_ref.shape[0]
    squares_ref[...] = jnp.zeros_like(squares_ref)

    def gate(g, _):
        lanes = lanes_of(g)
        place = place_of(g, rows)
        gated = query_side_ref[:, lanes] * (
            conv_ref[place, :] + skip_ref[:, lanes] * mix_ref[place, :]
        )
        summed = (residual_ref[:, lanes].astype(jnp.float32) + gated).astype(jnp.bfloat16)
        summed_ref[:, lanes] = summed
        widened = summed.astype(jnp.float32)
        squares_ref[0:rows, :] += widened * widened
        return 0

    lax.fori_loop(0, groups, gate, 0)
    row_squares = jnp.sum(jnp.transpose(squares_ref[...]), axis=0, keepdims=True)
    squares_out[...] = jnp.broadcast_to(row_squares, (8, padded))
    chan_copies = [
        pltpu.make_async_remote_copy(
            src_ref=squares_out,
            dst_ref=squares_in.at[j],
            send_sem=chan_send.at[j],
            recv_sem=chan_recv.at[j],
            device_id={"chan": chan_peers[j]},
            device_id_type=MESH,
        )
        for j in range(chan_size - 1)
    ]
    for copy in chan_copies:
        copy.start()
    for copy in chan_copies:
        copy.wait()
    together = squares_out[...]
    for j in range(chan_size - 1):
        together = together + squares_in[j]
    inverse = lax.rsqrt(together * (1.0 / D) + epsilon)
    squares_ref[...] = jnp.transpose(jnp.broadcast_to(inverse[0:1, :], (LANES, padded)))

    def normalize(g, _):
        lanes = lanes_of(g)
        widened = summed_ref[:, lanes].astype(jnp.float32)
        normed_ref[:, lanes] = (
            widened * squares_ref[0:rows, :] * gain_ref[:, lanes]
        ).astype(jnp.bfloat16)
        return 0

    lax.fori_loop(0, groups, normalize, 0)


def body(
    seq_size,
    chan_size,
    residual,
    query_in,
    key_in,
    value_in,
    short_filter,
    decay_rate,
    residue,
    skip_gain,
    norm_gain,
):
    rows, width = residual.shape
    poles = decay_rate.shape[0]
    groups = width // LANES
    levels = seq_size.bit_length() - 1
    padded = -(-rows // LANES) * LANES
    vmem = pl.BlockSpec(memory_space=pltpu.VMEM)
    f32, bf16 = jnp.float32, jnp.bfloat16
    by_channel = (poles, groups, LANES)
    return pl.pallas_call(
        functools.partial(kernel, seq_size, chan_size),
        out_shape=(jax.ShapeDtypeStruct((rows, width), bf16),) * 2,
        in_specs=[vmem] * 9,
        out_specs=(vmem, vmem),
        scratch_shapes=[
            pltpu.VMEM((groups * (rows + 8), LANES), f32),
            pltpu.VMEM((groups * (rows + 8), LANES), f32),
            pltpu.VMEM((rows, width), f32),
            pltpu.VMEM((groups * poles, LANES), f32),
            pltpu.VMEM(by_channel, f32),
            pltpu.VMEM(by_channel, f32),
            pltpu.VMEM(by_channel, f32),
            pltpu.VMEM(by_channel, f32),
            pltpu.VMEM(by_channel, f32),
            pltpu.VMEM((8, width), f32),
            pltpu.VMEM((8, width), f32),
            pltpu.VMEM((levels,) + by_channel, bf16),
            pltpu.VMEM((levels,) + by_channel, bf16),
            pltpu.VMEM((padded, LANES), f32),
            pltpu.VMEM((8, padded), f32),
            pltpu.VMEM((chan_size - 1, 8, padded), f32),
            pltpu.SemaphoreType.DMA((2,)),
            pltpu.SemaphoreType.DMA((levels,)),
            pltpu.SemaphoreType.DMA((levels,)),
            pltpu.SemaphoreType.DMA((chan_size - 1,)),
            pltpu.SemaphoreType.DMA((chan_size - 1,)),
        ],
        compiler_params=pltpu.CompilerParams(
            collective_id=0, has_side_effects=True, vmem_limit_bytes=40 * 1024 * 1024
        ),
    )(
        residual,
        query_in,
        key_in,
        value_in,
        short_filter,
        decay_rate,
        residue,
        skip_gain[None],
        norm_gain[None],
    )


def solution(mesh):
    in_specs = (
        P("seq", "chan"),
        P("seq", "chan"),
        P("seq", "chan"),
        P("seq", "chan"),
        P(None, None, "chan"),
        P(None, "chan"),
        P(None, "chan"),
        P("chan"),
        P("chan"),
    )
    out_specs = (P("seq", "chan"), P("seq", "chan"))
    return jax.shard_map(
        functools.partial(body, mesh.shape["seq"], mesh.shape["chan"]),
        mesh=mesh,
        in_specs=in_specs,
        out_specs=out_specs,
        check_vma=False,
    )
```

```python
import functools

import jax
import jax.numpy as jnp
from jax import lax
from jax.experimental import pallas as pl
from jax.experimental.pallas import tpu as pltpu
from jax.sharding import PartitionSpec as P

D = 8192
LANES = 128
epsilon = 1e-06
MESH = pl.DeviceIdType.MESH


def tree_sum(terms):
    while len(terms) > 1:
        paired = [terms[i] + terms[i + 1] for i in range(0, len(terms) - 1, 2)]
        if len(terms) % 2:
            paired.append(terms[-1])
        terms = paired
    return terms[0]


def kernel(
    seq_size,
    chan_size,
    residual_hbm,
    query_hbm,
    key_hbm,
    value_hbm,
    filter_hbm,
    decay_hbm,
    residue_hbm,
    skip_hbm,
    summed_hbm,
    inverse_hbm,
    summed_ref,
    inverse_ref,
    store_sem,
    residual_ref,
    query_ref,
    key_ref,
    value_ref,
    filter_ref,
    decay_ref,
    residue_ref,
    skip_ref,
    ends_ref,
    load_sem,
    mix_ref,
    conv_ref,
    query_side_ref,
    stage_ref,
    rate_ref,
    factor_ref,
    weight_ref,
    total_ref,
    carried_ref,
    tail_out,
    tail_in,
    state_out,
    state_in,
    squares_ref,
    squares_out,
    squares_in,
    tail_sem,
    state_send,
    state_recv,
    chan_send,
    chan_recv,
):
    rows, width = residual_ref.shape
    poles = decay_ref.shape[0]
    groups = width // LANES
    halves = groups // 8
    pitch = rows + 8
    levels = seq_size.bit_length() - 1
    me = lax.axis_index("seq")
    my_chan = lax.axis_index("chan")
    after = lax.rem(me + 1, seq_size)
    previous = lax.rem(me + seq_size - 1, seq_size)
    partners = [
        me + (1 - 2 * lax.rem(lax.div(me, 1 << k), 2)) * (1 << k) for k in range(levels)
    ]
    chan_peers = [lax.rem(my_chan + j, chan_size) for j in range(1, chan_size)]

    barrier = pltpu.get_barrier_semaphore()
    for other in [after, previous] + partners:
        pl.semaphore_signal(barrier, inc=1, device_id={"seq": other}, device_id_type=MESH)
    for other in chan_peers:
        pl.semaphore_signal(barrier, inc=1, device_id={"chan": other}, device_id_type=MESH)

    inputs = (query_ref, key_ref, value_ref)
    sources = (query_hbm, key_hbm, value_hbm)
    pairs = [(sources[i].at[rows - 16 : rows, :], ends_ref.at[i]) for i in range(3)] + [
        (decay_hbm, decay_ref),
        (residue_hbm, residue_ref),
        (filter_hbm, filter_ref),
        (key_hbm, key_ref),
        (value_hbm, value_ref),
        (query_hbm, query_ref),
        (residual_hbm, residual_ref),
        (skip_hbm, skip_ref),
    ]
    loads = [
        pltpu.make_async_copy(source, target, load_sem.at[i])
        for i, (source, target) in enumerate(pairs)
    ]
    for load in loads:
        load.start()
    for load in loads[:3]:
        load.wait()
    for i in range(3):
        last = ends_ref[i].astype(jnp.float32)
        tail_out[2 * i : 2 * i + 2, :] = last[14:16, :]
    tail_out[6:8, :] = jnp.zeros((2, width), jnp.float32)
    pl.semaphore_wait(barrier, 2 + levels + chan_size - 1)
    tail_copy = pltpu.make_async_remote_copy(
        src_ref=tail_out,
        dst_ref=tail_in,
        send_sem=tail_sem.at[0],
        recv_sem=tail_sem.at[1],
        device_id={"seq": after},
        device_id_type=MESH,
    )
    tail_copy.start()

    def to_channels(source, target):
        for g in range(groups):
            stage_ref[g * poles : (g + 1) * poles, :] = source[:, g * LANES : (g + 1) * LANES]
        for p in range(poles):
            for h in range(halves):
                target[p, h * 8 : h * 8 + 8, :] = stage_ref[
                    pl.ds(h * 8 * poles + p, 8, stride=poles), :
                ]

    for load in loads[3:5]:
        load.wait()
    to_channels(decay_ref, rate_ref)
    to_channels(residue_ref, weight_ref)
    rate = rate_ref[...]
    factor_ref[...] = jnp.exp(-rate)
    weight_ref[...] = weight_ref[...] * jnp.sqrt(2.0 * rate)

    def feature(i, count, lanes, tail):
        block = inputs[i][0:count, lanes].astype(jnp.float32)
        once = pltpu.roll(block, 1, 0)
        twice = pltpu.roll(block, 2, 0)
        if tail is not None:
            row = lax.broadcasted_iota(jnp.int32, (count, LANES), 0)
            older = tail[2 * i : 2 * i + 1, :]
            newer = tail[2 * i + 1 : 2 * i + 2, :]
            once = jnp.where(row == 0, newer, once)
            twice = jnp.where(row == 0, older, jnp.where(row == 1, newer, twice))
        taps = filter_ref[i, :, lanes]
        return taps[0:1, :] * block + taps[1:2, :] * once + taps[2:3, :] * twice

    def lanes_of(g):
        return pl.ds(pl.multiple_of(g * LANES, LANES), LANES)

    def place_of(g, count):
        return pl.ds(pl.multiple_of(g * pitch, 8), count)

    def mix_all(g, _):
        lanes = lanes_of(g)
        mix_ref[place_of(g, rows), :] = feature(1, rows, lanes, None) * feature(
            2, rows, lanes, None
        )
        return 0

    for load in loads[5:8]:
        load.wait()
    lax.fori_loop(0, groups, mix_all, 0)
    tail_copy.wait()
    is_first = me == 0

    def mix_first(g, _):
        lanes = lanes_of(g)
        tail = jnp.where(is_first, 0.0, tail_in[:, lanes])
        product = feature(1, 16, lanes, tail) * feature(2, 16, lanes, tail)
        mix_ref[place_of(g, 8), :] = product[0:8, :]
        return 0

    lax.fori_loop(0, groups, mix_first, 0)

    def half_of(ref, h):
        return tuple(ref[p, h * 8 : h * 8 + 8, :] for p in range(poles))

    def token(h, t):
        return pl.ds(h * 8 * pitch + t, 8, stride=pitch)

    zeros = (jnp.zeros((8, LANES), jnp.float32),) * poles
    for h in range(halves):
        factor = half_of(factor_ref, h)

        def advance(t, state, h=h, factor=factor):
            current = mix_ref[token(h, t), :]
            return tuple(a * s + current for a, s in zip(factor, state))

        state = lax.fori_loop(0, rows, advance, zeros, unroll=8)
        for p in range(poles):
            total_ref[p, h * 8 : h * 8 + 8, :] = state[p]

    def state_copy(k):
        return pltpu.make_async_remote_copy(
            src_ref=state_out.at[k],
            dst_ref=state_in.at[k],
            send_sem=state_send.at[k],
            recv_sem=state_recv.at[k],
            device_id={"seq": partners[k]},
            device_id_type=MESH,
        )

    def query_all(g, _):
        lanes = lanes_of(g)
        tail = jnp.where(is_first, 0.0, tail_in[:, lanes])
        query_side_ref[:, lanes] = feature(0, rows, lanes, tail)
        return 0

    def local_half(h):
        factor = half_of(factor_ref, h)

        def advance(t, state):
            current = mix_ref[token(h, t), :]
            state = tuple(a * s + current for a, s in zip(factor, state))
            conv_ref[token(h, t), :] = tree_sum(
                [weight_ref[p, h * 8 : h * 8 + 8, :] * state[p] for p in range(poles)]
            )
            return state

        lax.fori_loop(0, rows, advance, zeros, unroll=8)

    def query_work():
        for load in loads[8:]:
            load.wait()
        lax.fori_loop(0, groups, query_all, 0)

    beside = {0: [query_work]}
    for h in range(halves):
        beside.setdefault(min(1 + h, levels - 1), []).append(functools.partial(local_half, h))
    carried_ref[...] = jnp.zeros_like(carried_ref)
    for k in range(levels):
        state_out[k] = total_ref[...].astype(jnp.bfloat16)
        copy = state_copy(k)
        copy.start()
        for work in beside.get(k, []):
            work()
        copy.wait()
        size = 1 << k
        inside = lax.rem(me, size)
        upper = lax.rem(lax.div(me, size), 2) == 1
        span = (rows * inside).astype(jnp.float32)
        rate = rate_ref[...]
        arrived = state_in[k].astype(jnp.float32)
        carried_ref[...] += jnp.where(upper, jnp.exp(-rate * span) * arrived, 0.0)
        if k < levels - 1:
            own = total_ref[...]
            early = jnp.where(upper, arrived, own)
            late = jnp.where(upper, own, arrived)
            total_ref[...] = late + jnp.exp(-rate * (rows * size)) * early

    for h in range(halves):
        factor = half_of(factor_ref, h)
        start = tuple(
            weight_ref[p, h * 8 : h * 8 + 8, :] * carried_ref[p, h * 8 : h * 8 + 8, :]
            for p in range(poles)
        )

        def across(t, state, h=h, factor=factor):
            state = tuple(a * s for a, s in zip(factor, state))
            conv_ref[token(h, t), :] = conv_ref[token(h, t), :] + tree_sum(list(state))
            return state

        lax.fori_loop(0, rows, across, start, unroll=8)

    padded = squares_ref.shape[0]
    squares_ref[...] = jnp.zeros_like(squares_ref)

    def gate(g, _):
        lanes = lanes_of(g)
        place = place_of(g, rows)
        gated = query_side_ref[:, lanes] * (
            conv_ref[place, :] + skip_ref[:, lanes] * mix_ref[place, :]
        )
        summed = (residual_ref[:, lanes].astype(jnp.float32) + gated).astype(jnp.bfloat16)
        summed_ref[:, lanes] = summed
        widened = summed.astype(jnp.float32)
        squares_ref[0:rows, :] += widened * widened
        return 0

    lax.fori_loop(0, groups, gate, 0)
    store_summed = pltpu.make_async_copy(summed_ref, summed_hbm, store_sem.at[0])
    store_summed.start()
    row_squares = jnp.sum(jnp.transpose(squares_ref[...]), axis=0, keepdims=True)
    squares_out[...] = jnp.broadcast_to(row_squares, (8, padded))
    chan_copies = [
        pltpu.make_async_remote_copy(
            src_ref=squares_out,
            dst_ref=squares_in.at[j],
            send_sem=chan_send.at[j],
            recv_sem=chan_recv.at[j],
            device_id={"chan": chan_peers[j]},
            device_id_type=MESH,
        )
        for j in range(chan_size - 1)
    ]
    for copy in chan_copies:
        copy.start()
    for copy in chan_copies:
        copy.wait()
    together = squares_out[...]
    for j in range(chan_size - 1):
        together = together + squares_in[j]
    inverse = lax.rsqrt(together * (1.0 / D) + epsilon)
    inverse_ref[...] = jnp.transpose(jnp.broadcast_to(inverse[0:1, :], (LANES, padded)))[
        0:rows, :
    ]
    store_inverse = pltpu.make_async_copy(inverse_ref, inverse_hbm, store_sem.at[1])
    store_inverse.start()
    store_summed.wait()
    store_inverse.wait()


def finish(
    summed_hbm,
    inverse_hbm,
    gain_hbm,
    summed_out,
    normed_out,
    summed_ref,
    inverse_ref,
    gain_ref,
    normed_ref,
    load_sem,
    piece_in,
    summed_sem,
    normed_sem,
):
    pieces, each, width = normed_ref.shape
    spans = [slice(piece * each, (piece + 1) * each) for piece in range(pieces)]
    loads = [
        pltpu.make_async_copy(inverse_hbm, inverse_ref, load_sem.at[0]),
        pltpu.make_async_copy(gain_hbm, gain_ref, load_sem.at[1]),
    ]
    arrivals = [
        pltpu.make_async_copy(summed_hbm.at[spans[i], :], summed_ref.at[i], piece_in.at[i])
        for i in range(pieces)
    ]
    for load in loads + arrivals:
        load.start()
    for load in loads:
        load.wait()
    stores = []
    for i in range(pieces):
        arrivals[i].wait()
        keep = pltpu.make_async_copy(
            summed_ref.at[i], summed_out.at[spans[i], :], summed_sem.at[i]
        )
        keep.start()
        for g in range(width // LANES):
            lanes = slice(g * LANES, (g + 1) * LANES)
            widened = summed_ref[i, :, lanes].astype(jnp.float32)
            normed_ref[i, :, lanes] = (
                widened * inverse_ref[spans[i], :] * gain_ref[:, lanes]
            ).astype(jnp.bfloat16)
        store = pltpu.make_async_copy(
            normed_ref.at[i], normed_out.at[spans[i], :], normed_sem.at[i]
        )
        store.start()
        stores += [keep, store]
    for store in stores:
        store.wait()


def body(
    seq_size,
    chan_size,
    residual,
    query_in,
    key_in,
    value_in,
    short_filter,
    decay_rate,
    residue,
    skip_gain,
    norm_gain,
):
    rows, width = residual.shape
    poles = decay_rate.shape[0]
    groups = width // LANES
    levels = seq_size.bit_length() - 1
    padded = -(-rows // LANES) * LANES
    f32, bf16 = jnp.float32, jnp.bfloat16
    by_channel = (poles, groups, LANES)
    hbm = pl.BlockSpec(memory_space=pltpu.HBM)
    whole = jax.ShapeDtypeStruct((rows, width), bf16)
    summed, inverse = pl.pallas_call(
        functools.partial(kernel, seq_size, chan_size),
        out_shape=(
            whole,
            jax.ShapeDtypeStruct((rows, LANES), f32),
        ),
        in_specs=[hbm] * 8,
        out_specs=(hbm, hbm),
        scratch_shapes=[
            pltpu.VMEM((rows, width), bf16),
            pltpu.VMEM((rows, LANES), f32),
            pltpu.SemaphoreType.DMA((2,)),
            pltpu.VMEM((rows, width), bf16),
            pltpu.VMEM((rows, width), bf16),
            pltpu.VMEM((rows, width), bf16),
            pltpu.VMEM((rows, width), bf16),
            pltpu.VMEM(short_filter.shape, f32),
            pltpu.VMEM((poles, width), f32),
            pltpu.VMEM((poles, width), f32),
            pltpu.VMEM((1, width), f32),
            pltpu.VMEM((3, 16, width), bf16),
            pltpu.SemaphoreType.DMA((11,)),
            pltpu.VMEM((groups * (rows + 8), LANES), f32),
            pltpu.VMEM((groups * (rows + 8), LANES), f32),
            pltpu.VMEM((rows, width), f32),
            pltpu.VMEM((groups * poles, LANES), f32),
            pltpu.VMEM(by_channel, f32),
            pltpu.VMEM(by_channel, f32),
            pltpu.VMEM(by_channel, f32),
            pltpu.VMEM(by_channel, f32),
            pltpu.VMEM(by_channel, f32),
            pltpu.VMEM((8, width), f32),
            pltpu.VMEM((8, width), f32),
            pltpu.VMEM((levels,) + by_channel, bf16),
            pltpu.VMEM((levels,) + by_channel, bf16),
            pltpu.VMEM((padded, LANES), f32),
            pltpu.VMEM((8, padded), f32),
            pltpu.VMEM((chan_size - 1, 8, padded), f32),
            pltpu.SemaphoreType.DMA((2,)),
            pltpu.SemaphoreType.DMA((levels,)),
            pltpu.SemaphoreType.DMA((levels,)),
            pltpu.SemaphoreType.DMA((chan_size - 1,)),
            pltpu.SemaphoreType.DMA((chan_size - 1,)),
        ],
        compiler_params=pltpu.CompilerParams(
            collective_id=0, has_side_effects=True, vmem_limit_bytes=58 * 1024 * 1024
        ),
    )(
        residual,
        query_in,
        key_in,
        value_in,
        short_filter,
        decay_rate,
        residue,
        skip_gain[None],
    )
    pieces = rows // 32
    return pl.pallas_call(
        finish,
        out_shape=(whole, whole),
        in_specs=[hbm] * 3,
        out_specs=(hbm, hbm),
        scratch_shapes=[
            pltpu.VMEM((pieces, 32, width), bf16),
            pltpu.VMEM((rows, LANES), f32),
            pltpu.VMEM((1, width), f32),
            pltpu.VMEM((pieces, 32, width), bf16),
            pltpu.SemaphoreType.DMA((2,)),
            pltpu.SemaphoreType.DMA((pieces,)),
            pltpu.SemaphoreType.DMA((pieces,)),
            pltpu.SemaphoreType.DMA((pieces,)),
        ],
        compiler_params=pltpu.CompilerParams(vmem_limit_bytes=58 * 1024 * 1024),
    )(summed, inverse, norm_gain[None])


def solution(mesh):
    in_specs = (
        P("seq", "chan"),
        P("seq", "chan"),
        P("seq", "chan"),
        P("seq", "chan"),
        P(None, None, "chan"),
        P(None, "chan"),
        P(None, "chan"),
        P("chan"),
        P("chan"),
    )
    out_specs = (P("seq", "chan"), P("seq", "chan"))
    return jax.shard_map(
        functools.partial(body, mesh.shape["seq"], mesh.shape["chan"]),
        mesh=mesh,
        in_specs=in_specs,
        out_specs=out_specs,
        check_vma=False,
    )
```

```python
import functools

import jax
import jax.numpy as jnp
from jax import lax
from jax.experimental import pallas as pl
from jax.experimental.pallas import tpu as pltpu
from jax.sharding import PartitionSpec as P

D = 8192
LANES = 128
epsilon = 1e-06
MESH = pl.DeviceIdType.MESH


def tree_sum(terms):
    while len(terms) > 1:
        paired = [terms[i] + terms[i + 1] for i in range(0, len(terms) - 1, 2)]
        if len(terms) % 2:
            paired.append(terms[-1])
        terms = paired
    return terms[0]


def radices_of(seq_size):
    radices = [2]
    rest = seq_size // 2
    while rest > 1:
        radices.append(4 if rest % 4 == 0 else 2)
        rest //= radices[-1]
    return radices


def kernel(
    seq_size,
    chan_size,
    residual_hbm,
    query_hbm,
    key_hbm,
    value_hbm,
    filter_hbm,
    decay_hbm,
    residue_hbm,
    skip_hbm,
    summed_hbm,
    inverse_hbm,
    summed_ref,
    inverse_ref,
    store_sem,
    residual_ref,
    query_ref,
    key_ref,
    value_ref,
    filter_ref,
    decay_ref,
    residue_ref,
    skip_ref,
    ends_ref,
    load_sem,
    mix_ref,
    conv_ref,
    query_side_ref,
    stage_ref,
    rate_ref,
    factor_ref,
    weight_ref,
    total_ref,
    carried_ref,
    tail_out,
    tail_in,
    state_out,
    state_in,
    squares_ref,
    squares_out,
    squares_in,
    tail_sem,
    state_send,
    state_recv,
    chan_send,
    chan_recv,
):
    rows, width = residual_ref.shape
    poles = decay_ref.shape[0]
    groups = width // LANES
    halves = groups // 8
    pitch = rows + 8
    radices = radices_of(seq_size)
    levels = len(radices)
    me = lax.axis_index("seq")
    my_chan = lax.axis_index("chan")
    after = lax.rem(me + 1, seq_size)
    previous = lax.rem(me + seq_size - 1, seq_size)
    sizes, digits, partners = [], [], []
    size = 1
    for radix in radices:
        digit = lax.rem(lax.div(me, size), radix)
        sizes.append(size)
        digits.append(digit)
        partners.append(
            [me + (lax.rem(digit + j, radix) - digit) * size for j in range(1, radix)]
        )
        size *= radix
    every_partner = [other for level in partners for other in level]
    chan_peers = [lax.rem(my_chan + j, chan_size) for j in range(1, chan_size)]

    barrier = pltpu.get_barrier_semaphore()
    for other in [after, previous] + every_partner:
        pl.semaphore_signal(barrier, inc=1, device_id={"seq": other}, device_id_type=MESH)
    for other in chan_peers:
        pl.semaphore_signal(barrier, inc=1, device_id={"chan": other}, device_id_type=MESH)

    inputs = (query_ref, key_ref, value_ref)
    sources = (query_hbm, key_hbm, value_hbm)
    pairs = [(sources[i].at[rows - 16 : rows, :], ends_ref.at[i]) for i in range(3)] + [
        (decay_hbm, decay_ref),
        (residue_hbm, residue_ref),
        (filter_hbm, filter_ref),
        (key_hbm, key_ref),
        (value_hbm, value_ref),
        (query_hbm, query_ref),
        (residual_hbm, residual_ref),
        (skip_hbm, skip_ref),
    ]
    loads = [
        pltpu.make_async_copy(source, target, load_sem.at[i])
        for i, (source, target) in enumerate(pairs)
    ]
    for load in loads:
        load.start()
    def to_channels(source, target):
        for g in range(groups):
            stage_ref[g * poles : (g + 1) * poles, :] = source[:, g * LANES : (g + 1) * LANES]
        for p in range(poles):
            for h in range(halves):
                target[p, h * 8 : h * 8 + 8, :] = stage_ref[
                    pl.ds(h * 8 * poles + p, 8, stride=poles), :
                ]

    for load in loads[3:5]:
        load.wait()
    to_channels(decay_ref, rate_ref)
    to_channels(residue_ref, weight_ref)
    rate = rate_ref[...]
    factor_ref[...] = jnp.exp(-rate)
    weight_ref[...] = weight_ref[...] * jnp.sqrt(2.0 * rate)

    def feature(i, count, lanes, tail):
        block = inputs[i][0:count, lanes].astype(jnp.float32)
        once = pltpu.roll(block, 1, 0)
        twice = pltpu.roll(block, 2, 0)
        if tail is not None:
            row = lax.broadcasted_iota(jnp.int32, (count, LANES), 0)
            older = tail[2 * i : 2 * i + 1, :]
            newer = tail[2 * i + 1 : 2 * i + 2, :]
            once = jnp.where(row == 0, newer, once)
            twice = jnp.where(row == 0, older, jnp.where(row == 1, newer, twice))
        taps = filter_ref[i, :, lanes]
        return taps[0:1, :] * block + taps[1:2, :] * once + taps[2:3, :] * twice

    def lanes_of(g):
        return pl.ds(pl.multiple_of(g * LANES, LANES), LANES)

    def place_of(g, count):
        return pl.ds(pl.multiple_of(g * pitch, 8), count)

    def mix_all(g, _):
        lanes = lanes_of(g)
        mix_ref[place_of(g, rows), :] = feature(1, rows, lanes, None) * feature(
            2, rows, lanes, None
        )
        mix_ref[place_of(g, 2), :] = jnp.zeros((2, LANES), jnp.float32)
        return 0

    for load in loads[5:8]:
        load.wait()
    lax.fori_loop(0, groups, mix_all, 0)
    for load in loads[:3]:
        load.wait()
    for i in range(3):
        last = ends_ref[i].astype(jnp.float32)
        tail_out[2 * i : 2 * i + 2, :] = last[14:16, :]
    tail_out[6:8, :] = jnp.zeros((2, width), jnp.float32)
    pl.semaphore_wait(barrier, 2 + len(every_partner) + chan_size - 1)
    tail_copy = pltpu.make_async_remote_copy(
        src_ref=tail_out,
        dst_ref=tail_in,
        send_sem=tail_sem.at[0],
        recv_sem=tail_sem.at[1],
        device_id={"seq": after},
        device_id_type=MESH,
    )
    tail_copy.start()

    def half_of(ref, h):
        return tuple(ref[p, h * 8 : h * 8 + 8, :] for p in range(poles))

    def token(h, t):
        return pl.ds(h * 8 * pitch + t, 8, stride=pitch)

    def first_tokens(t):
        return jnp.concatenate([mix_ref[token(h, t), :] for h in range(halves)], axis=0)[None]

    zeros = (jnp.zeros((8, LANES), jnp.float32),) * poles
    for h in range(halves):
        factor = half_of(factor_ref, h)

        def advance(t, state, h=h, factor=factor):
            current = mix_ref[token(h, t), :]
            return tuple(a * s + current for a, s in zip(factor, state))

        state = lax.fori_loop(0, rows, advance, zeros, unroll=8)
        for p in range(poles):
            total_ref[p, h * 8 : h * 8 + 8, :] = state[p]

    tail_copy.wait()
    is_first = me == 0

    def mix_first(g, _):
        lanes = lanes_of(g)
        tail = jnp.where(is_first, 0.0, tail_in[:, lanes])
        product = feature(1, 16, lanes, tail) * feature(2, 16, lanes, tail)
        mix_ref[place_of(g, 8), :] = product[0:8, :]
        return 0

    lax.fori_loop(0, groups, mix_first, 0)

    reach = jnp.exp(-rate_ref[...] * (rows - 2.0))
    total_ref[...] = total_ref[...] + reach * (factor_ref[...] * first_tokens(0) + first_tokens(1))

    slots = {}
    for k in range(levels):
        for j in range(1, radices[k]):
            slots[k, j] = len(slots)

    def state_copy(k, j):
        return pltpu.make_async_remote_copy(
            src_ref=state_out.at[k],
            dst_ref=state_in.at[slots[k, j]],
            send_sem=state_send.at[slots[k, j]],
            recv_sem=state_recv.at[slots[k, j]],
            device_id={"seq": partners[k][j - 1]},
            device_id_type=MESH,
        )

    def query_all(g, _):
        lanes = lanes_of(g)
        tail = jnp.where(is_first, 0.0, tail_in[:, lanes])
        query_side_ref[:, lanes] = feature(0, rows, lanes, tail)
        return 0

    def local_half(h):
        factor = half_of(factor_ref, h)

        def advance(t, state):
            current = mix_ref[token(h, t), :]
            state = tuple(a * s + current for a, s in zip(factor, state))
            conv_ref[token(h, t), :] = tree_sum(
                [weight_ref[p, h * 8 : h * 8 + 8, :] * state[p] for p in range(poles)]
            )
            return state

        lax.fori_loop(0, rows, advance, zeros, unroll=8)

    def query_work():
        for load in loads[8:]:
            load.wait()
        lax.fori_loop(0, groups, query_all, 0)

    beside = {0: [query_work]}
    for h in range(halves):
        beside.setdefault(min(1 + h, levels - 1), []).append(functools.partial(local_half, h))
    carried_ref[...] = jnp.zeros_like(carried_ref)
    for k in range(levels):
        state_out[k] = total_ref[...].astype(jnp.bfloat16)
        radix, size, digit = radices[k], sizes[k], digits[k]
        final = k == levels - 1
        copies = [state_copy(k, j) for j in range(1, radix)]
        for j, copy in enumerate(copies, 1):
            if final:
                pl.when(digit + j < radix)(copy.start)
            else:
                copy.start()
        for work in beside.get(k, []):
            work()
        inside = lax.rem(me, size)
        if not final:
            ahead = (rows * size * (radix - 1 - digit)).astype(jnp.float32)
            grown = jnp.exp(-rate_ref[...] * ahead) * total_ref[...]
        for j, copy in enumerate(copies, 1):

            def absorb(k=k, j=j, size=size, inside=inside):
                span = (rows * (inside + size * (j - 1))).astype(jnp.float32)
                carried_ref[...] += jnp.exp(-rate_ref[...] * span) * state_in[
                    slots[k, j]
                ].astype(jnp.float32)

            if final:

                def receive(copy=copy, absorb=absorb):
                    copy.wait_recv()
                    absorb()

                pl.when(digit >= j)(receive)
            else:
                copy.wait_recv()
                pl.when(digit >= j)(absorb)
                ahead = (
                    rows * size * (radix - 1 - lax.rem(digit - j + radix, radix))
                ).astype(jnp.float32)
                grown = grown + jnp.exp(-rate_ref[...] * ahead) * state_in[
                    slots[k, j]
                ].astype(jnp.float32)
        if not final:
            total_ref[...] = grown

    for h in range(halves):
        factor = half_of(factor_ref, h)
        start = tuple(
            weight_ref[p, h * 8 : h * 8 + 8, :] * carried_ref[p, h * 8 : h * 8 + 8, :]
            for p in range(poles)
        )

        def across(t, state, h=h, factor=factor):
            state = tuple(a * s for a, s in zip(factor, state))
            conv_ref[token(h, t), :] = conv_ref[token(h, t), :] + tree_sum(list(state))
            return state

        lax.fori_loop(0, rows, across, start, unroll=8)

    for k in range(levels):
        for j in range(1, radices[k]):
            if k == levels - 1:
                pl.when(digits[k] + j < radices[k])(state_copy(k, j).wait_send)
            else:
                state_copy(k, j).wait_send()

    padded = squares_ref.shape[0]
    squares_ref[...] = jnp.zeros_like(squares_ref)

    def gate(g, _):
        lanes = lanes_of(g)
        place = place_of(g, rows)
        gated = query_side_ref[:, lanes] * (
            conv_ref[place, :] + skip_ref[:, lanes] * mix_ref[place, :]
        )
        summed = (residual_ref[:, lanes].astype(jnp.float32) + gated).astype(jnp.bfloat16)
        summed_ref[:, lanes] = summed
        widened = summed.astype(jnp.float32)
        squares_ref[0:rows, :] += widened * widened
        return 0

    lax.fori_loop(0, groups, gate, 0)
    store_summed = pltpu.make_async_copy(summed_ref, summed_hbm, store_sem.at[0])
    store_summed.start()
    row_squares = jnp.sum(jnp.transpose(squares_ref[...]), axis=0, keepdims=True)
    squares_out[...] = jnp.broadcast_to(row_squares, (8, padded))
    chan_copies = [
        pltpu.make_async_remote_copy(
            src_ref=squares_out,
            dst_ref=squares_in.at[j],
            send_sem=chan_send.at[j],
            recv_sem=chan_recv.at[j],
            device_id={"chan": chan_peers[j]},
            device_id_type=MESH,
        )
        for j in range(chan_size - 1)
    ]
    for copy in chan_copies:
        copy.start()
    for copy in chan_copies:
        copy.wait()
    together = squares_out[...]
    for j in range(chan_size - 1):
        together = together + squares_in[j]
    inverse = lax.rsqrt(together * (1.0 / D) + epsilon)
    inverse_ref[...] = jnp.transpose(jnp.broadcast_to(inverse[0:1, :], (LANES, padded)))[
        0:rows, :
    ]
    store_inverse = pltpu.make_async_copy(inverse_ref, inverse_hbm, store_sem.at[1])
    store_inverse.start()
    store_summed.wait()
    store_inverse.wait()


def finish(
    summed_hbm,
    inverse_hbm,
    gain_hbm,
    summed_out,
    normed_out,
    summed_ref,
    inverse_ref,
    gain_ref,
    normed_ref,
    load_sem,
    piece_in,
    summed_sem,
    normed_sem,
):
    pieces, each, width = normed_ref.shape
    spans = [slice(piece * each, (piece + 1) * each) for piece in range(pieces)]
    loads = [
        pltpu.make_async_copy(inverse_hbm, inverse_ref, load_sem.at[0]),
        pltpu.make_async_copy(gain_hbm, gain_ref, load_sem.at[1]),
    ]
    arrivals = [
        pltpu.make_async_copy(summed_hbm.at[spans[i], :], summed_ref.at[i], piece_in.at[i])
        for i in range(pieces)
    ]
    for load in loads + arrivals:
        load.start()
    for load in loads:
        load.wait()
    stores = []
    for i in range(pieces):
        arrivals[i].wait()
        keep = pltpu.make_async_copy(
            summed_ref.at[i], summed_out.at[spans[i], :], summed_sem.at[i]
        )
        keep.start()
        for g in range(width // LANES):
            lanes = slice(g * LANES, (g + 1) * LANES)
            widened = summed_ref[i, :, lanes].astype(jnp.float32)
            normed_ref[i, :, lanes] = (
                widened * inverse_ref[spans[i], :] * gain_ref[:, lanes]
            ).astype(jnp.bfloat16)
        store = pltpu.make_async_copy(
            normed_ref.at[i], normed_out.at[spans[i], :], normed_sem.at[i]
        )
        store.start()
        stores += [keep, store]
    for store in stores:
        store.wait()


def body(
    seq_size,
    chan_size,
    residual,
    query_in,
    key_in,
    value_in,
    short_filter,
    decay_rate,
    residue,
    skip_gain,
    norm_gain,
):
    rows, width = residual.shape
    poles = decay_rate.shape[0]
    groups = width // LANES
    radices = radices_of(seq_size)
    levels = len(radices)
    slots = sum(radices) - levels
    padded = -(-rows // LANES) * LANES
    f32, bf16 = jnp.float32, jnp.bfloat16
    by_channel = (poles, groups, LANES)
    hbm = pl.BlockSpec(memory_space=pltpu.HBM)
    whole = jax.ShapeDtypeStruct((rows, width), bf16)
    summed, inverse = pl.pallas_call(
        functools.partial(kernel, seq_size, chan_size),
        out_shape=(
            whole,
            jax.ShapeDtypeStruct((rows, LANES), f32),
        ),
        in_specs=[hbm] * 8,
        out_specs=(hbm, hbm),
        scratch_shapes=[
            pltpu.VMEM((rows, width), bf16),
            pltpu.VMEM((rows, LANES), f32),
            pltpu.SemaphoreType.DMA((2,)),
            pltpu.VMEM((rows, width), bf16),
            pltpu.VMEM((rows, width), bf16),
            pltpu.VMEM((rows, width), bf16),
            pltpu.VMEM((rows, width), bf16),
            pltpu.VMEM(short_filter.shape, f32),
            pltpu.VMEM((poles, width), f32),
            pltpu.VMEM((poles, width), f32),
            pltpu.VMEM((1, width), f32),
            pltpu.VMEM((3, 16, width), bf16),
            pltpu.SemaphoreType.DMA((11,)),
            pltpu.VMEM((groups * (rows + 8), LANES), f32),
            pltpu.VMEM((groups * (rows + 8), LANES), f32),
            pltpu.VMEM((rows, width), f32),
            pltpu.VMEM((groups * poles, LANES), f32),
            pltpu.VMEM(by_channel, f32),
            pltpu.VMEM(by_channel, f32),
            pltpu.VMEM(by_channel, f32),
            pltpu.VMEM(by_channel, f32),
            pltpu.VMEM(by_channel, f32),
            pltpu.VMEM((8, width), f32),
            pltpu.VMEM((8, width), f32),
            pltpu.VMEM((levels,) + by_channel, bf16),
            pltpu.VMEM((slots,) + by_channel, bf16),
            pltpu.VMEM((padded, LANES), f32),
            pltpu.VMEM((8, padded), f32),
            pltpu.VMEM((chan_size - 1, 8, padded), f32),
            pltpu.SemaphoreType.DMA((2,)),
            pltpu.SemaphoreType.DMA((slots,)),
            pltpu.SemaphoreType.DMA((slots,)),
            pltpu.SemaphoreType.DMA((chan_size - 1,)),
            pltpu.SemaphoreType.DMA((chan_size - 1,)),
        ],
        compiler_params=pltpu.CompilerParams(
            collective_id=0, has_side_effects=True, vmem_limit_bytes=58 * 1024 * 1024
        ),
    )(
        residual,
        query_in,
        key_in,
        value_in,
        short_filter,
        decay_rate,
        residue,
        skip_gain[None],
    )
    pieces = rows // 32
    return pl.pallas_call(
        finish,
        out_shape=(whole, whole),
        in_specs=[hbm] * 3,
        out_specs=(hbm, hbm),
        scratch_shapes=[
            pltpu.VMEM((pieces, 32, width), bf16),
            pltpu.VMEM((rows, LANES), f32),
            pltpu.VMEM((1, width), f32),
            pltpu.VMEM((pieces, 32, width), bf16),
            pltpu.SemaphoreType.DMA((2,)),
            pltpu.SemaphoreType.DMA((pieces,)),
            pltpu.SemaphoreType.DMA((pieces,)),
            pltpu.SemaphoreType.DMA((pieces,)),
        ],
        compiler_params=pltpu.CompilerParams(vmem_limit_bytes=58 * 1024 * 1024),
    )(summed, inverse, norm_gain[None])


def solution(mesh):
    in_specs = (
        P("seq", "chan"),
        P("seq", "chan"),
        P("seq", "chan"),
        P("seq", "chan"),
        P(None, None, "chan"),
        P(None, "chan"),
        P(None, "chan"),
        P("chan"),
        P("chan"),
    )
    out_specs = (P("seq", "chan"), P("seq", "chan"))
    return jax.shard_map(
        functools.partial(body, mesh.shape["seq"], mesh.shape["chan"]),
        mesh=mesh,
        in_specs=in_specs,
        out_specs=out_specs,
        check_vma=False,
    )
```

```python
import functools

import jax
import jax.numpy as jnp
from jax import lax
from jax.experimental import pallas as pl
from jax.experimental.pallas import tpu as pltpu
from jax.sharding import PartitionSpec as P

D = 8192
LANES = 128
epsilon = 1e-06
MESH = pl.DeviceIdType.MESH


def tree_sum(terms):
    while len(terms) > 1:
        paired = [terms[i] + terms[i + 1] for i in range(0, len(terms) - 1, 2)]
        if len(terms) % 2:
            paired.append(terms[-1])
        terms = paired
    return terms[0]


def radices_of(seq_size):
    radices = [2]
    rest = seq_size // 2
    while rest > 1:
        radices.append(4 if rest % 4 == 0 else 2)
        rest //= radices[-1]
    return radices


def kernel(
    seq_size,
    chan_size,
    residual_hbm,
    query_hbm,
    key_hbm,
    value_hbm,
    filter_hbm,
    decay_hbm,
    residue_hbm,
    skip_hbm,
    summed_hbm,
    inverse_hbm,
    summed_ref,
    inverse_ref,
    store_sem,
    residual_ref,
    query_ref,
    key_ref,
    value_ref,
    filter_ref,
    decay_ref,
    residue_ref,
    skip_ref,
    ends_ref,
    load_sem,
    mix_ref,
    conv_ref,
    query_side_ref,
    stage_ref,
    rate_ref,
    factor_ref,
    weight_ref,
    total_ref,
    carried_ref,
    tail_out,
    tail_in,
    state_out,
    state_in,
    squares_ref,
    squares_out,
    squares_in,
    tail_sem,
    state_send,
    state_recv,
    chan_send,
    chan_recv,
):
    rows, width = residual_ref.shape
    poles = decay_ref.shape[0]
    groups = width // LANES
    halves = groups // 8
    pitch = rows + 8
    radices = radices_of(seq_size)
    levels = len(radices)
    me = lax.axis_index("seq")
    my_chan = lax.axis_index("chan")
    after = lax.rem(me + 1, seq_size)
    previous = lax.rem(me + seq_size - 1, seq_size)
    sizes, digits, partners = [], [], []
    size = 1
    for radix in radices:
        digit = lax.rem(lax.div(me, size), radix)
        sizes.append(size)
        digits.append(digit)
        partners.append(
            [me + (lax.rem(digit + j, radix) - digit) * size for j in range(1, radix)]
        )
        size *= radix
    every_partner = [other for level in partners for other in level]
    chan_peers = [lax.rem(my_chan + j, chan_size) for j in range(1, chan_size)]

    barrier = pltpu.get_barrier_semaphore()
    for other in [after, previous] + every_partner:
        pl.semaphore_signal(barrier, inc=1, device_id={"seq": other}, device_id_type=MESH)
    for other in chan_peers:
        pl.semaphore_signal(barrier, inc=1, device_id={"chan": other}, device_id_type=MESH)

    inputs = (query_ref, key_ref, value_ref)
    sources = (query_hbm, key_hbm, value_hbm)
    pairs = [(sources[i].at[rows - 16 : rows, :], ends_ref.at[i]) for i in range(3)] + [
        (decay_hbm, decay_ref),
        (residue_hbm, residue_ref),
        (filter_hbm, filter_ref),
        (key_hbm, key_ref),
        (value_hbm, value_ref),
        (query_hbm, query_ref),
        (residual_hbm, residual_ref),
        (skip_hbm, skip_ref),
    ]
    loads = [
        pltpu.make_async_copy(source, target, load_sem.at[i])
        for i, (source, target) in enumerate(pairs)
    ]
    for load in loads:
        load.start()
    def to_channels(source, target):
        for g in range(groups):
            stage_ref[g * poles : (g + 1) * poles, :] = source[:, g * LANES : (g + 1) * LANES]
        for p in range(poles):
            for h in range(halves):
                target[p, h * 8 : h * 8 + 8, :] = stage_ref[
                    pl.ds(h * 8 * poles + p, 8, stride=poles), :
                ]

    for load in loads[3:5]:
        load.wait()
    to_channels(decay_ref, rate_ref)
    to_channels(residue_ref, weight_ref)
    rate = rate_ref[...]
    factor_ref[...] = jnp.exp(-rate)
    weight_ref[...] = weight_ref[...] * jnp.sqrt(2.0 * rate)

    def feature(i, count, lanes, tail):
        block = inputs[i][0:count, lanes].astype(jnp.float32)
        once = pltpu.roll(block, 1, 0)
        twice = pltpu.roll(block, 2, 0)
        if tail is not None:
            row = lax.broadcasted_iota(jnp.int32, (count, LANES), 0)
            older = tail[2 * i : 2 * i + 1, :]
            newer = tail[2 * i + 1 : 2 * i + 2, :]
            once = jnp.where(row == 0, newer, once)
            twice = jnp.where(row == 0, older, jnp.where(row == 1, newer, twice))
        taps = filter_ref[i, :, lanes]
        return taps[0:1, :] * block + taps[1:2, :] * once + taps[2:3, :] * twice

    def lanes_of(g):
        return pl.ds(pl.multiple_of(g * LANES, LANES), LANES)

    def place_of(g, count):
        return pl.ds(pl.multiple_of(g * pitch, 8), count)

    def mix_all(g, _):
        lanes = lanes_of(g)
        mix_ref[place_of(g, rows), :] = feature(1, rows, lanes, None) * feature(
            2, rows, lanes, None
        )
        mix_ref[place_of(g, 2), :] = jnp.zeros((2, LANES), jnp.float32)
        return 0

    for load in loads[:3]:
        load.wait()
    for i in range(3):
        last = ends_ref[i].astype(jnp.float32)
        tail_out[2 * i : 2 * i + 2, :] = last[14:16, :]
    tail_out[6:8, :] = jnp.zeros((2, width), jnp.float32)
    pl.semaphore_wait(barrier, 2 + len(every_partner) + chan_size - 1)
    tail_copy = pltpu.make_async_remote_copy(
        src_ref=tail_out,
        dst_ref=tail_in,
        send_sem=tail_sem.at[0],
        recv_sem=tail_sem.at[1],
        device_id={"seq": after},
        device_id_type=MESH,
    )
    tail_copy.start()
    for load in loads[5:8]:
        load.wait()
    lax.fori_loop(0, groups, mix_all, 0)

    def half_of(ref, h):
        return tuple(ref[p, h * 8 : h * 8 + 8, :] for p in range(poles))

    def token(h, t):
        return pl.ds(h * 8 * pitch + t, 8, stride=pitch)

    def first_tokens(t):
        return jnp.concatenate([mix_ref[token(h, t), :] for h in range(halves)], axis=0)[None]

    zeros = (jnp.zeros((8, LANES), jnp.float32),) * poles
    for h in range(halves):
        factor = half_of(factor_ref, h)

        def advance(t, state, h=h, factor=factor):
            current = mix_ref[token(h, t), :]
            return tuple(a * s + current for a, s in zip(factor, state))

        state = lax.fori_loop(0, rows, advance, zeros, unroll=8)
        for p in range(poles):
            total_ref[p, h * 8 : h * 8 + 8, :] = state[p]

    tail_copy.wait()
    is_first = me == 0

    def mix_first(g, _):
        lanes = lanes_of(g)
        tail = jnp.where(is_first, 0.0, tail_in[:, lanes])
        product = feature(1, 16, lanes, tail) * feature(2, 16, lanes, tail)
        mix_ref[place_of(g, 8), :] = product[0:8, :]
        return 0

    lax.fori_loop(0, groups, mix_first, 0)

    reach = jnp.exp(-rate_ref[...] * (rows - 2.0))
    total_ref[...] = total_ref[...] + reach * (factor_ref[...] * first_tokens(0) + first_tokens(1))

    slots = {}
    for k in range(levels):
        for j in range(1, radices[k]):
            slots[k, j] = len(slots)

    def state_copy(k, j):
        return pltpu.make_async_remote_copy(
            src_ref=state_out.at[k],
            dst_ref=state_in.at[slots[k, j]],
            send_sem=state_send.at[slots[k, j]],
            recv_sem=state_recv.at[slots[k, j]],
            device_id={"seq": partners[k][j - 1]},
            device_id_type=MESH,
        )

    def query_all(g, _):
        lanes = lanes_of(g)
        tail = jnp.where(is_first, 0.0, tail_in[:, lanes])
        query_side_ref[:, lanes] = feature(0, rows, lanes, tail)
        return 0

    def local_half(h):
        factor = half_of(factor_ref, h)

        def advance(t, state):
            current = mix_ref[token(h, t), :]
            state = tuple(a * s + current for a, s in zip(factor, state))
            conv_ref[token(h, t), :] = tree_sum(
                [weight_ref[p, h * 8 : h * 8 + 8, :] * state[p] for p in range(poles)]
            )
            return state

        lax.fori_loop(0, rows, advance, zeros, unroll=8)

    def query_work():
        for load in loads[8:]:
            load.wait()
        lax.fori_loop(0, groups, query_all, 0)

    beside = {0: [query_work]}
    for h in range(halves):
        beside.setdefault(min(1 + h, levels - 1), []).append(functools.partial(local_half, h))
    carried_ref[...] = jnp.zeros_like(carried_ref)
    for k in range(levels):
        state_out[k] = total_ref[...].astype(jnp.bfloat16)
        radix, size, digit = radices[k], sizes[k], digits[k]
        final = k == levels - 1
        copies = [state_copy(k, j) for j in range(1, radix)]
        for j, copy in enumerate(copies, 1):
            if final:
                pl.when(digit + j < radix)(copy.start)
            else:
                copy.start()
        for work in beside.get(k, []):
            work()
        inside = lax.rem(me, size)
        if not final:
            ahead = (rows * size * (radix - 1 - digit)).astype(jnp.float32)
            grown = jnp.exp(-rate_ref[...] * ahead) * total_ref[...]
        for j, copy in enumerate(copies, 1):

            def absorb(k=k, j=j, size=size, inside=inside):
                span = (rows * (inside + size * (j - 1))).astype(jnp.float32)
                carried_ref[...] += jnp.exp(-rate_ref[...] * span) * state_in[
                    slots[k, j]
                ].astype(jnp.float32)

            if final:

                def receive(copy=copy, absorb=absorb):
                    copy.wait_recv()
                    absorb()

                pl.when(digit >= j)(receive)
            else:
                copy.wait_recv()
                pl.when(digit >= j)(absorb)
                ahead = (
                    rows * size * (radix - 1 - lax.rem(digit - j + radix, radix))
                ).astype(jnp.float32)
                grown = grown + jnp.exp(-rate_ref[...] * ahead) * state_in[
                    slots[k, j]
                ].astype(jnp.float32)
        if not final:
            total_ref[...] = grown

    for h in range(halves):
        factor = half_of(factor_ref, h)
        start = tuple(
            weight_ref[p, h * 8 : h * 8 + 8, :] * carried_ref[p, h * 8 : h * 8 + 8, :]
            for p in range(poles)
        )

        def across(t, state, h=h, factor=factor):
            state = tuple(a * s for a, s in zip(factor, state))
            conv_ref[token(h, t), :] = conv_ref[token(h, t), :] + tree_sum(list(state))
            return state

        lax.fori_loop(0, rows, across, start, unroll=8)

    for k in range(levels):
        for j in range(1, radices[k]):
            if k == levels - 1:
                pl.when(digits[k] + j < radices[k])(state_copy(k, j).wait_send)
            else:
                state_copy(k, j).wait_send()

    padded = squares_ref.shape[0]
    squares_ref[...] = jnp.zeros_like(squares_ref)

    def gate(g, _):
        lanes = lanes_of(g)
        place = place_of(g, rows)
        gated = query_side_ref[:, lanes] * (
            conv_ref[place, :] + skip_ref[:, lanes] * mix_ref[place, :]
        )
        summed = (residual_ref[:, lanes].astype(jnp.float32) + gated).astype(jnp.bfloat16)
        summed_ref[:, lanes] = summed
        widened = summed.astype(jnp.float32)
        squares_ref[0:rows, :] += widened * widened
        return 0

    lax.fori_loop(0, groups, gate, 0)
    row_squares = jnp.sum(jnp.transpose(squares_ref[...]), axis=0, keepdims=True)
    squares_out[...] = jnp.broadcast_to(row_squares, (8, padded))
    chan_copies = [
        pltpu.make_async_remote_copy(
            src_ref=squares_out,
            dst_ref=squares_in.at[j],
            send_sem=chan_send.at[j],
            recv_sem=chan_recv.at[j],
            device_id={"chan": chan_peers[j]},
            device_id_type=MESH,
        )
        for j in range(chan_size - 1)
    ]
    for copy in chan_copies:
        copy.start()
    store_summed = pltpu.make_async_copy(summed_ref, summed_hbm, store_sem.at[0])
    store_summed.start()
    for copy in chan_copies:
        copy.wait()
    together = squares_out[...]
    for j in range(chan_size - 1):
        together = together + squares_in[j]
    inverse = lax.rsqrt(together * (1.0 / D) + epsilon)
    inverse_ref[...] = jnp.transpose(jnp.broadcast_to(inverse[0:1, :], (LANES, padded)))[
        0:rows, :
    ]
    store_inverse = pltpu.make_async_copy(inverse_ref, inverse_hbm, store_sem.at[1])
    store_inverse.start()
    store_summed.wait()
    store_inverse.wait()


def finish(
    summed_hbm,
    inverse_hbm,
    gain_hbm,
    summed_out,
    normed_out,
    summed_ref,
    inverse_ref,
    gain_ref,
    normed_ref,
    load_sem,
    piece_in,
    summed_sem,
    normed_sem,
):
    pieces, each, width = normed_ref.shape
    spans = [slice(piece * each, (piece + 1) * each) for piece in range(pieces)]
    loads = [
        pltpu.make_async_copy(inverse_hbm, inverse_ref, load_sem.at[0]),
        pltpu.make_async_copy(gain_hbm, gain_ref, load_sem.at[1]),
    ]
    arrivals = [
        pltpu.make_async_copy(summed_hbm.at[spans[i], :], summed_ref.at[i], piece_in.at[i])
        for i in range(pieces)
    ]
    for load in loads + arrivals:
        load.start()
    for load in loads:
        load.wait()
    stores = []
    for i in range(pieces):
        arrivals[i].wait()
        keep = pltpu.make_async_copy(
            summed_ref.at[i], summed_out.at[spans[i], :], summed_sem.at[i]
        )
        keep.start()
        for g in range(width // LANES):
            lanes = slice(g * LANES, (g + 1) * LANES)
            widened = summed_ref[i, :, lanes].astype(jnp.float32)
            normed_ref[i, :, lanes] = (
                widened * inverse_ref[spans[i], :] * gain_ref[:, lanes]
            ).astype(jnp.bfloat16)
        store = pltpu.make_async_copy(
            normed_ref.at[i], normed_out.at[spans[i], :], normed_sem.at[i]
        )
        store.start()
        stores += [keep, store]
    for store in stores:
        store.wait()


def body(
    seq_size,
    chan_size,
    residual,
    query_in,
    key_in,
    value_in,
    short_filter,
    decay_rate,
    residue,
    skip_gain,
    norm_gain,
):
    rows, width = residual.shape
    poles = decay_rate.shape[0]
    groups = width // LANES
    radices = radices_of(seq_size)
    levels = len(radices)
    slots = sum(radices) - levels
    padded = -(-rows // LANES) * LANES
    f32, bf16 = jnp.float32, jnp.bfloat16
    by_channel = (poles, groups, LANES)
    hbm = pl.BlockSpec(memory_space=pltpu.HBM)
    whole = jax.ShapeDtypeStruct((rows, width), bf16)
    summed, inverse = pl.pallas_call(
        functools.partial(kernel, seq_size, chan_size),
        out_shape=(
            whole,
            jax.ShapeDtypeStruct((rows, LANES), f32),
        ),
        in_specs=[hbm] * 8,
        out_specs=(hbm, hbm),
        scratch_shapes=[
            pltpu.VMEM((rows, width), bf16),
            pltpu.VMEM((rows, LANES), f32),
            pltpu.SemaphoreType.DMA((2,)),
            pltpu.VMEM((rows, width), bf16),
            pltpu.VMEM((rows, width), bf16),
            pltpu.VMEM((rows, width), bf16),
            pltpu.VMEM((rows, width), bf16),
            pltpu.VMEM(short_filter.shape, f32),
            pltpu.VMEM((poles, width), f32),
            pltpu.VMEM((poles, width), f32),
            pltpu.VMEM((1, width), f32),
            pltpu.VMEM((3, 16, width), bf16),
            pltpu.SemaphoreType.DMA((11,)),
            pltpu.VMEM((groups * (rows + 8), LANES), f32),
            pltpu.VMEM((groups * (rows + 8), LANES), f32),
            pltpu.VMEM((rows, width), f32),
            pltpu.VMEM((groups * poles, LANES), f32),
            pltpu.VMEM(by_channel, f32),
            pltpu.VMEM(by_channel, f32),
            pltpu.VMEM(by_channel, f32),
            pltpu.VMEM(by_channel, f32),
            pltpu.VMEM(by_channel, f32),
            pltpu.VMEM((8, width), f32),
            pltpu.VMEM((8, width), f32),
            pltpu.VMEM((levels,) + by_channel, bf16),
            pltpu.VMEM((slots,) + by_channel, bf16),
            pltpu.VMEM((padded, LANES), f32),
            pltpu.VMEM((8, padded), f32),
            pltpu.VMEM((chan_size - 1, 8, padded), f32),
            pltpu.SemaphoreType.DMA((2,)),
            pltpu.SemaphoreType.DMA((slots,)),
            pltpu.SemaphoreType.DMA((slots,)),
            pltpu.SemaphoreType.DMA((chan_size - 1,)),
            pltpu.SemaphoreType.DMA((chan_size - 1,)),
        ],
        compiler_params=pltpu.CompilerParams(
            collective_id=0, has_side_effects=True, vmem_limit_bytes=58 * 1024 * 1024
        ),
    )(
        residual,
        query_in,
        key_in,
        value_in,
        short_filter,
        decay_rate,
        residue,
        skip_gain[None],
    )
    pieces = rows // 32
    return pl.pallas_call(
        finish,
        out_shape=(whole, whole),
        in_specs=[hbm] * 3,
        out_specs=(hbm, hbm),
        scratch_shapes=[
            pltpu.VMEM((pieces, 32, width), bf16),
            pltpu.VMEM((rows, LANES), f32),
            pltpu.VMEM((1, width), f32),
            pltpu.VMEM((pieces, 32, width), bf16),
            pltpu.SemaphoreType.DMA((2,)),
            pltpu.SemaphoreType.DMA((pieces,)),
            pltpu.SemaphoreType.DMA((pieces,)),
            pltpu.SemaphoreType.DMA((pieces,)),
        ],
        compiler_params=pltpu.CompilerParams(vmem_limit_bytes=58 * 1024 * 1024),
    )(summed, inverse, norm_gain[None])


def solution(mesh):
    in_specs = (
        P("seq", "chan"),
        P("seq", "chan"),
        P("seq", "chan"),
        P("seq", "chan"),
        P(None, None, "chan"),
        P(None, "chan"),
        P(None, "chan"),
        P("chan"),
        P("chan"),
    )
    out_specs = (P("seq", "chan"), P("seq", "chan"))
    return jax.shard_map(
        functools.partial(body, mesh.shape["seq"], mesh.shape["chan"]),
        mesh=mesh,
        in_specs=in_specs,
        out_specs=out_specs,
        check_vma=False,
    )
```

```python
import functools

import jax
import jax.numpy as jnp
from jax import lax
from jax.experimental import pallas as pl
from jax.experimental.pallas import tpu as pltpu
from jax.sharding import PartitionSpec as P

D = 8192
LANES = 128
epsilon = 1e-06
MESH = pl.DeviceIdType.MESH


def tree_sum(terms):
    while len(terms) > 1:
        paired = [terms[i] + terms[i + 1] for i in range(0, len(terms) - 1, 2)]
        if len(terms) % 2:
            paired.append(terms[-1])
        terms = paired
    return terms[0]


def radices_of(seq_size):
    radices = [2]
    rest = seq_size // 2
    while rest > 1:
        radices.append(4 if rest % 4 == 0 else 2)
        rest //= radices[-1]
    return radices


def kernel(
    seq_size,
    chan_size,
    residual_hbm,
    query_hbm,
    key_hbm,
    value_hbm,
    filter_hbm,
    decay_hbm,
    residue_hbm,
    skip_hbm,
    summed_hbm,
    inverse_hbm,
    summed_ref,
    inverse_ref,
    store_sem,
    residual_ref,
    query_ref,
    key_ref,
    value_ref,
    filter_ref,
    decay_ref,
    residue_ref,
    skip_ref,
    ends_ref,
    load_sem,
    mix_ref,
    conv_ref,
    query_side_ref,
    stage_ref,
    rate_ref,
    factor_ref,
    weight_ref,
    total_ref,
    carried_ref,
    tail_out,
    tail_in,
    state_out,
    state_in,
    squares_ref,
    squares_out,
    squares_in,
    tail_sem,
    state_send,
    state_recv,
    chan_send,
    chan_recv,
):
    rows, width = residual_ref.shape
    poles = decay_ref.shape[0]
    groups = width // LANES
    halves = groups // 8
    pitch = rows + 8
    radices = radices_of(seq_size)
    levels = len(radices)
    me = lax.axis_index("seq")
    my_chan = lax.axis_index("chan")
    after = lax.rem(me + 1, seq_size)
    previous = lax.rem(me + seq_size - 1, seq_size)
    sizes, digits, partners = [], [], []
    size = 1
    for radix in radices:
        digit = lax.rem(lax.div(me, size), radix)
        sizes.append(size)
        digits.append(digit)
        partners.append(
            [me + (lax.rem(digit + j, radix) - digit) * size for j in range(1, radix)]
        )
        size *= radix
    every_partner = [other for level in partners for other in level]
    chan_peers = [lax.rem(my_chan + j, chan_size) for j in range(1, chan_size)]

    barrier = pltpu.get_barrier_semaphore()
    for other in [after, previous] + every_partner:
        pl.semaphore_signal(barrier, inc=1, device_id={"seq": other}, device_id_type=MESH)
    for other in chan_peers:
        pl.semaphore_signal(barrier, inc=1, device_id={"chan": other}, device_id_type=MESH)

    inputs = (query_ref, key_ref, value_ref)
    sources = (query_hbm, key_hbm, value_hbm)
    pairs = [(sources[i].at[rows - 16 : rows, :], ends_ref.at[i]) for i in range(3)] + [
        (decay_hbm, decay_ref),
        (residue_hbm, residue_ref),
        (filter_hbm, filter_ref),
        (key_hbm, key_ref),
        (value_hbm, value_ref),
        (query_hbm, query_ref),
        (residual_hbm, residual_ref),
        (skip_hbm, skip_ref),
    ]
    loads = [
        pltpu.make_async_copy(source, target, load_sem.at[i])
        for i, (source, target) in enumerate(pairs)
    ]
    for load in loads:
        load.start()
    def to_channels(source, target):
        for g in range(groups):
            stage_ref[g * poles : (g + 1) * poles, :] = source[:, g * LANES : (g + 1) * LANES]
        for p in range(poles):
            for h in range(halves):
                target[p, h * 8 : h * 8 + 8, :] = stage_ref[
                    pl.ds(h * 8 * poles + p, 8, stride=poles), :
                ]

    for load in loads[3:5]:
        load.wait()
    to_channels(decay_ref, rate_ref)
    to_channels(residue_ref, weight_ref)
    rate = rate_ref[...]
    factor_ref[...] = jnp.exp(-rate)
    weight_ref[...] = weight_ref[...] * jnp.sqrt(2.0 * rate)

    def feature(i, count, lanes, tail):
        block = inputs[i][0:count, lanes].astype(jnp.float32)
        once = pltpu.roll(block, 1, 0)
        twice = pltpu.roll(block, 2, 0)
        if tail is not None:
            row = lax.broadcasted_iota(jnp.int32, (count, LANES), 0)
            older = tail[2 * i : 2 * i + 1, :]
            newer = tail[2 * i + 1 : 2 * i + 2, :]
            once = jnp.where(row == 0, newer, once)
            twice = jnp.where(row == 0, older, jnp.where(row == 1, newer, twice))
        taps = filter_ref[i, :, lanes]
        return taps[0:1, :] * block + taps[1:2, :] * once + taps[2:3, :] * twice

    def lanes_of(g):
        return pl.ds(pl.multiple_of(g * LANES, LANES), LANES)

    def place_of(g, count):
        return pl.ds(pl.multiple_of(g * pitch, 8), count)

    def mix_all(g, _):
        lanes = lanes_of(g)
        mix_ref[place_of(g, rows), :] = feature(1, rows, lanes, None) * feature(
            2, rows, lanes, None
        )
        mix_ref[place_of(g, 2), :] = jnp.zeros((2, LANES), jnp.float32)
        return 0

    for load in loads[:3]:
        load.wait()
    for i in range(3):
        last = ends_ref[i].astype(jnp.float32)
        tail_out[2 * i : 2 * i + 2, :] = last[14:16, :]
    tail_out[6:8, :] = jnp.zeros((2, width), jnp.float32)
    pl.semaphore_wait(barrier, 2 + len(every_partner) + chan_size - 1)
    tail_copy = pltpu.make_async_remote_copy(
        src_ref=tail_out,
        dst_ref=tail_in,
        send_sem=tail_sem.at[0],
        recv_sem=tail_sem.at[1],
        device_id={"seq": after},
        device_id_type=MESH,
    )
    tail_copy.start()
    for load in loads[5:8]:
        load.wait()
    lax.fori_loop(0, groups, mix_all, 0, unroll=2)

    def half_of(ref, h):
        return tuple(ref[p, h * 8 : h * 8 + 8, :] for p in range(poles))

    def token(h, t):
        return pl.ds(h * 8 * pitch + t, 8, stride=pitch)

    def first_tokens(t):
        return jnp.concatenate([mix_ref[token(h, t), :] for h in range(halves)], axis=0)[None]

    zeros = (jnp.zeros((8, LANES), jnp.float32),) * poles
    for h in range(halves):
        factor = half_of(factor_ref, h)

        def advance(t, state, h=h, factor=factor):
            current = mix_ref[token(h, t), :]
            return tuple(a * s + current for a, s in zip(factor, state))

        state = lax.fori_loop(0, rows, advance, zeros, unroll=16)
        for p in range(poles):
            total_ref[p, h * 8 : h * 8 + 8, :] = state[p]

    tail_copy.wait()
    is_first = me == 0

    def mix_first(g, _):
        lanes = lanes_of(g)
        tail = jnp.where(is_first, 0.0, tail_in[:, lanes])
        product = feature(1, 16, lanes, tail) * feature(2, 16, lanes, tail)
        mix_ref[place_of(g, 8), :] = product[0:8, :]
        return 0

    lax.fori_loop(0, groups, mix_first, 0, unroll=4)

    reach = jnp.exp(-rate_ref[...] * (rows - 2.0))
    total_ref[...] = total_ref[...] + reach * (factor_ref[...] * first_tokens(0) + first_tokens(1))

    slots = {}
    for k in range(levels):
        for j in range(1, radices[k]):
            slots[k, j] = len(slots)

    def state_copy(k, j):
        return pltpu.make_async_remote_copy(
            src_ref=state_out.at[k],
            dst_ref=state_in.at[slots[k, j]],
            send_sem=state_send.at[slots[k, j]],
            recv_sem=state_recv.at[slots[k, j]],
            device_id={"seq": partners[k][j - 1]},
            device_id_type=MESH,
        )

    def query_all(g, _):
        lanes = lanes_of(g)
        tail = jnp.where(is_first, 0.0, tail_in[:, lanes])
        query_side_ref[:, lanes] = feature(0, rows, lanes, tail)
        return 0

    def local_half(h):
        factor = half_of(factor_ref, h)

        def advance(t, state):
            current = mix_ref[token(h, t), :]
            state = tuple(a * s + current for a, s in zip(factor, state))
            conv_ref[token(h, t), :] = tree_sum(
                [weight_ref[p, h * 8 : h * 8 + 8, :] * state[p] for p in range(poles)]
            )
            return state

        lax.fori_loop(0, rows, advance, zeros, unroll=16)

    def query_work():
        for load in loads[8:]:
            load.wait()
        lax.fori_loop(0, groups, query_all, 0, unroll=2)

    beside = {0: [query_work]}
    for h in range(halves):
        beside.setdefault(min(1 + h, levels - 1), []).append(functools.partial(local_half, h))
    carried_ref[...] = jnp.zeros_like(carried_ref)
    for k in range(levels):
        state_out[k] = total_ref[...].astype(jnp.bfloat16)
        radix, size, digit = radices[k], sizes[k], digits[k]
        final = k == levels - 1
        copies = [state_copy(k, j) for j in range(1, radix)]
        for j, copy in enumerate(copies, 1):
            if final:
                pl.when(digit + j < radix)(copy.start)
            else:
                copy.start()
        for work in beside.get(k, []):
            work()
        inside = lax.rem(me, size)
        if not final:
            ahead = (rows * size * (radix - 1 - digit)).astype(jnp.float32)
            grown = jnp.exp(-rate_ref[...] * ahead) * total_ref[...]
        for j, copy in enumerate(copies, 1):

            def absorb(k=k, j=j, size=size, inside=inside):
                span = (rows * (inside + size * (j - 1))).astype(jnp.float32)
                carried_ref[...] += jnp.exp(-rate_ref[...] * span) * state_in[
                    slots[k, j]
                ].astype(jnp.float32)

            if final:

                def receive(copy=copy, absorb=absorb):
                    copy.wait_recv()
                    absorb()

                pl.when(digit >= j)(receive)
            else:
                copy.wait_recv()
                pl.when(digit >= j)(absorb)
                ahead = (
                    rows * size * (radix - 1 - lax.rem(digit - j + radix, radix))
                ).astype(jnp.float32)
                grown = grown + jnp.exp(-rate_ref[...] * ahead) * state_in[
                    slots[k, j]
                ].astype(jnp.float32)
        if not final:
            total_ref[...] = grown

    for h in range(halves):
        factor = half_of(factor_ref, h)
        start = tuple(
            weight_ref[p, h * 8 : h * 8 + 8, :] * carried_ref[p, h * 8 : h * 8 + 8, :]
            for p in range(poles)
        )

        def across(t, state, h=h, factor=factor):
            state = tuple(a * s for a, s in zip(factor, state))
            conv_ref[token(h, t), :] = conv_ref[token(h, t), :] + tree_sum(list(state))
            return state

        lax.fori_loop(0, rows, across, start, unroll=16)

    for k in range(levels):
        for j in range(1, radices[k]):
            if k == levels - 1:
                pl.when(digits[k] + j < radices[k])(state_copy(k, j).wait_send)
            else:
                state_copy(k, j).wait_send()

    padded = squares_ref.shape[0]
    squares_ref[...] = jnp.zeros_like(squares_ref)

    def gate(g, _):
        lanes = lanes_of(g)
        place = place_of(g, rows)
        gated = query_side_ref[:, lanes] * (
            conv_ref[place, :] + skip_ref[:, lanes] * mix_ref[place, :]
        )
        summed = (residual_ref[:, lanes].astype(jnp.float32) + gated).astype(jnp.bfloat16)
        summed_ref[:, lanes] = summed
        widened = summed.astype(jnp.float32)
        squares_ref[0:rows, :] += widened * widened
        return 0

    lax.fori_loop(0, groups, gate, 0, unroll=2)
    row_squares = jnp.sum(jnp.transpose(squares_ref[...]), axis=0, keepdims=True)
    squares_out[...] = jnp.broadcast_to(row_squares, (8, padded))
    chan_copies = [
        pltpu.make_async_remote_copy(
            src_ref=squares_out,
            dst_ref=squares_in.at[j],
            send_sem=chan_send.at[j],
            recv_sem=chan_recv.at[j],
            device_id={"chan": chan_peers[j]},
            device_id_type=MESH,
        )
        for j in range(chan_size - 1)
    ]
    for copy in chan_copies:
        copy.start()
    store_summed = pltpu.make_async_copy(summed_ref, summed_hbm, store_sem.at[0])
    store_summed.start()
    for copy in chan_copies:
        copy.wait()
    together = squares_out[...]
    for j in range(chan_size - 1):
        together = together + squares_in[j]
    inverse = lax.rsqrt(together * (1.0 / D) + epsilon)
    inverse_ref[...] = jnp.transpose(jnp.broadcast_to(inverse[0:1, :], (LANES, padded)))[
        0:rows, :
    ]
    store_inverse = pltpu.make_async_copy(inverse_ref, inverse_hbm, store_sem.at[1])
    store_inverse.start()
    store_summed.wait()
    store_inverse.wait()


def finish(
    summed_hbm,
    inverse_hbm,
    gain_hbm,
    summed_out,
    normed_out,
    summed_ref,
    inverse_ref,
    gain_ref,
    normed_ref,
    load_sem,
    piece_in,
    summed_sem,
    normed_sem,
):
    pieces, each, width = normed_ref.shape
    spans = [slice(piece * each, (piece + 1) * each) for piece in range(pieces)]
    loads = [
        pltpu.make_async_copy(inverse_hbm, inverse_ref, load_sem.at[0]),
        pltpu.make_async_copy(gain_hbm, gain_ref, load_sem.at[1]),
    ]
    arrivals = [
        pltpu.make_async_copy(summed_hbm.at[spans[i], :], summed_ref.at[i], piece_in.at[i])
        for i in range(pieces)
    ]
    for load in loads + arrivals:
        load.start()
    for load in loads:
        load.wait()
    stores = []
    for i in range(pieces):
        arrivals[i].wait()
        keep = pltpu.make_async_copy(
            summed_ref.at[i], summed_out.at[spans[i], :], summed_sem.at[i]
        )
        keep.start()
        for g in range(width // LANES):
            lanes = slice(g * LANES, (g + 1) * LANES)
            widened = summed_ref[i, :, lanes].astype(jnp.float32)
            normed_ref[i, :, lanes] = (
                widened * inverse_ref[spans[i], :] * gain_ref[:, lanes]
            ).astype(jnp.bfloat16)
        store = pltpu.make_async_copy(
            normed_ref.at[i], normed_out.at[spans[i], :], normed_sem.at[i]
        )
        store.start()
        stores += [keep, store]
    for store in stores:
        store.wait()


def body(
    seq_size,
    chan_size,
    residual,
    query_in,
    key_in,
    value_in,
    short_filter,
    decay_rate,
    residue,
    skip_gain,
    norm_gain,
):
    rows, width = residual.shape
    poles = decay_rate.shape[0]
    groups = width // LANES
    radices = radices_of(seq_size)
    levels = len(radices)
    slots = sum(radices) - levels
    padded = -(-rows // LANES) * LANES
    f32, bf16 = jnp.float32, jnp.bfloat16
    by_channel = (poles, groups, LANES)
    hbm = pl.BlockSpec(memory_space=pltpu.HBM)
    whole = jax.ShapeDtypeStruct((rows, width), bf16)
    summed, inverse = pl.pallas_call(
        functools.partial(kernel, seq_size, chan_size),
        out_shape=(
            whole,
            jax.ShapeDtypeStruct((rows, LANES), f32),
        ),
        in_specs=[hbm] * 8,
        out_specs=(hbm, hbm),
        scratch_shapes=[
            pltpu.VMEM((rows, width), bf16),
            pltpu.VMEM((rows, LANES), f32),
            pltpu.SemaphoreType.DMA((2,)),
            pltpu.VMEM((rows, width), bf16),
            pltpu.VMEM((rows, width), bf16),
            pltpu.VMEM((rows, width), bf16),
            pltpu.VMEM((rows, width), bf16),
            pltpu.VMEM(short_filter.shape, f32),
            pltpu.VMEM((poles, width), f32),
            pltpu.VMEM((poles, width), f32),
            pltpu.VMEM((1, width), f32),
            pltpu.VMEM((3, 16, width), bf16),
            pltpu.SemaphoreType.DMA((11,)),
            pltpu.VMEM((groups * (rows + 8), LANES), f32),
            pltpu.VMEM((groups * (rows + 8), LANES), f32),
            pltpu.VMEM((rows, width), f32),
            pltpu.VMEM((groups * poles, LANES), f32),
            pltpu.VMEM(by_channel, f32),
            pltpu.VMEM(by_channel, f32),
            pltpu.VMEM(by_channel, f32),
            pltpu.VMEM(by_channel, f32),
            pltpu.VMEM(by_channel, f32),
            pltpu.VMEM((8, width), f32),
            pltpu.VMEM((8, width), f32),
            pltpu.VMEM((levels,) + by_channel, bf16),
            pltpu.VMEM((slots,) + by_channel, bf16),
            pltpu.VMEM((padded, LANES), f32),
            pltpu.VMEM((8, padded), f32),
            pltpu.VMEM((chan_size - 1, 8, padded), f32),
            pltpu.SemaphoreType.DMA((2,)),
            pltpu.SemaphoreType.DMA((slots,)),
            pltpu.SemaphoreType.DMA((slots,)),
            pltpu.SemaphoreType.DMA((chan_size - 1,)),
            pltpu.SemaphoreType.DMA((chan_size - 1,)),
        ],
        compiler_params=pltpu.CompilerParams(
            collective_id=0, has_side_effects=True, vmem_limit_bytes=58 * 1024 * 1024
        ),
    )(
        residual,
        query_in,
        key_in,
        value_in,
        short_filter,
        decay_rate,
        residue,
        skip_gain[None],
    )
    pieces = rows // 32
    return pl.pallas_call(
        finish,
        out_shape=(whole, whole),
        in_specs=[hbm] * 3,
        out_specs=(hbm, hbm),
        scratch_shapes=[
            pltpu.VMEM((pieces, 32, width), bf16),
            pltpu.VMEM((rows, LANES), f32),
            pltpu.VMEM((1, width), f32),
            pltpu.VMEM((pieces, 32, width), bf16),
            pltpu.SemaphoreType.DMA((2,)),
            pltpu.SemaphoreType.DMA((pieces,)),
            pltpu.SemaphoreType.DMA((pieces,)),
            pltpu.SemaphoreType.DMA((pieces,)),
        ],
        compiler_params=pltpu.CompilerParams(vmem_limit_bytes=58 * 1024 * 1024),
    )(summed, inverse, norm_gain[None])


def solution(mesh):
    in_specs = (
        P("seq", "chan"),
        P("seq", "chan"),
        P("seq", "chan"),
        P("seq", "chan"),
        P(None, None, "chan"),
        P(None, "chan"),
        P(None, "chan"),
        P("chan"),
        P("chan"),
    )
    out_specs = (P("seq", "chan"), P("seq", "chan"))
    return jax.shard_map(
        functools.partial(body, mesh.shape["seq"], mesh.shape["chan"]),
        mesh=mesh,
        in_specs=in_specs,
        out_specs=out_specs,
        check_vma=False,
    )
```
